128 devices in a mesh: row: 8 (over x, z_hi), col: 16 (over y, z_lo, core).
Axes of the slice: x: 4, y: 4, z: 4 (z_hi: 2, z_lo: 2; z = z_hi * 2 + z_lo), core: 2. Of those that a mesh axis runs over, the one named last changes fastest.
Arguments:
- tokens: bfloat16 [512, 16384], P(('row', 'col')), may hold values from -6 to 6
- gate_weight: bfloat16 [16384, 26624], P('col', 'row'), may hold values from -0.046875 to 0.046875
- up_weight: bfloat16 [16384, 26624], P('col', 'row'), may hold values from -0.046875 to 0.046875
- down_weight: bfloat16 [26624, 16384], P('row', 'col'), may hold values from -0.0390625 to 0.0390625
Outputs:
- mixed: bfloat16 [512, 16384], P('row', 'col')
The draws below stay inside these ranges and needn't reach their ends.
All inputs are finite; a program needn't handle non-finite values.
Results may differ from the reference program's by a relative error of at most 0.005.
Values may be sent and summed in bfloat16 or wider, within the bound.
No kernel may reach another device: no remote copies, remote signals or barrier semaphores. Data moves between devices by JAX's collectives and lax.ppermute only.
A program may use at most 128 MiB of HBM per device.

```python
import jax
import jax.numpy as jnp

D = 16384
FF = 26624
TOKENS = 512


def block_levels(own_key, shape, pieces, least, top_value):
    def one(position, blocks):
        draws = jax.random.uniform(jax.random.fold_in(jax.random.fold_in(own_key, 6), position), (blocks,), jnp.float32, least / len(pieces), top_value / len(pieces))
        return jnp.repeat(jnp.exp(draws), shape[position] // blocks).reshape((-1,) + (1,) * (len(shape) - position - 1))

    loudness = one(*pieces[0])
    for cut in pieces[1:]:
        loudness = loudness * one(*cut)
    return loudness


def normal_values(own_key, extent, deviation, most, split=(), held_as=jnp.bfloat16):
    loudness = block_levels(own_key, extent, split, -0.22, 0.18) if split else 1.0
    entries = jax.random.normal(own_key, extent, jnp.float32) * deviation * loudness
    return jnp.minimum(jnp.maximum(entries, -most), most).astype(held_as)


def setup_inputs(seed: int = 0) -> dict:
    key_of = jax.random.split(jax.random.key(seed), 5)
    tokens = normal_values(key_of[0], (TOKENS, D), 1.0, 6.0, ((0, 128),))
    gate_weight = normal_values(key_of[1], (D, FF), D ** -0.5, 0.046875, ((0, 16), (1, 8)))
    up_weight = normal_values(key_of[2], (D, FF), D ** -0.5, 0.046875, ((0, 16), (1, 8)))
    down_weight = normal_values(key_of[3], (FF, D), FF ** -0.5, 0.0390625, ((0, 8), (1, 16)))
    return {"tokens": tokens, "gate_weight": gate_weight, "up_weight": up_weight, "down_weight": down_weight}


def reference(tokens, gate_weight, up_weight, down_weight):
    gate_value = jnp.dot(tokens, gate_weight, preferred_element_type=jnp.float32)
    up_value = jnp.dot(tokens, up_weight, preferred_element_type=jnp.float32)
    hidden = (jax.nn.silu(gate_value) * up_value).astype(jnp.bfloat16)
    return jnp.dot(hidden, down_weight, preferred_element_type=jnp.float32).astype(jnp.bfloat16)
```

```python
import jax
import jax.numpy as jnp
from jax import lax
from jax.sharding import PartitionSpec as P

F32, BF16, F16 = jnp.float32, jnp.bfloat16, jnp.float16
LIFT = 8.0
CHUNKS = ((2, 1), (3, 0))


def along(axis, size, move):
    pairs = [(i, move(i)) for i in range(size)]
    return lambda v: lax.ppermute(v, axis, pairs)


def lifted(v):
    return (v * LIFT).astype(F16)


def lowered(v):
    return v.astype(F32) * (1 / LIFT)


def per_device(tokens, gate_weight, up_weight, down_weight):
    row, col = lax.axis_index("row"), lax.axis_index("col")
    z_hi, x = row % 2, row // 2
    core, z_lo, y = col % 2, (col // 2) % 2, col // 4
    to_core = along("col", 16, lambda c: c ^ 1)
    to_z = along("col", 16, lambda c: c ^ 2)
    y_up = along("col", 16, lambda c: (c + 4) % 16)
    y_down = along("col", 16, lambda c: (c + 12) % 16)

    features = tokens.shape[1] // 16
    blocks = tokens.reshape(4, 16, features).transpose(1, 0, 2).reshape(1, 64, features)
    blocks = jnp.broadcast_to(blocks, (8, 64, features)).reshape(512, features)
    every = lax.all_to_all(blocks, ("row", "col"), split_axis=0, concat_axis=0, tiled=True)
    every = every.reshape(4, 2, 4, 16, features)

    def tokens_of(j, half):
        block = lax.dynamic_slice(
            every, ((x + j) % 4, half, 0, 0, 0), (1, 1, 4, 16, features)
        ).reshape(4, 16, features)
        doubled = jnp.concatenate((block, block), axis=0)
        return lax.dynamic_slice_in_dim(doubled, y, 4, 0)

    half_hidden = gate_weight.shape[1] // 2
    arrived = []
    for chunk in CHUNKS:
        n = 16 * len(chunk)

        def rows_of(half):
            parts = [tokens_of(j, half) for j in chunk]
            return jnp.stack(parts, axis=1).reshape(4 * n, features)

        away, kept = rows_of(1 - core), rows_of(core)

        def project(weight):
            sent = to_core(lifted(jnp.dot(away, weight, preferred_element_type=F32)))
            return jnp.dot(kept, weight, preferred_element_type=F32) + lowered(sent)

        gate, up = project(gate_weight), project(up_weight)
        g = [gate[n * k : n * (k + 1)] for k in range(4)]
        u = [up[n * k : n * (k + 1)] for k in range(4)]
        first_up = y_up(jnp.stack((lifted(g[2]), lifted(u[1]))))
        first_down = y_down(jnp.stack((lifted(u[2]), lifted(g[3]))))
        second_up = y_up(lifted(g[1] + lowered(first_up[0])))
        second_down = y_down(lifted(u[3] + lowered(first_down[0])))
        gate = g[0] + lowered(first_down[1]) + lowered(second_up)
        up = u[0] + lowered(first_up[1]) + lowered(second_down)
        both = jnp.stack((gate, up))
        lo, hi = both[:, :, :half_hidden], both[:, :, half_hidden:]
        beside = to_z(lifted(jnp.where(z_lo == 0, hi, lo)))
        total = jnp.where(z_lo == 0, lo, hi) + lowered(beside)
        hidden = (jax.nn.silu(total[0]) * total[1]).astype(BF16)
        beside = to_z(hidden)
        hidden = jnp.concatenate(
            (jnp.where(z_lo == 0, hidden, beside), jnp.where(z_lo == 0, beside, hidden)), axis=1
        )
        from_below, from_above = y_up(hidden), y_down(hidden)
        far_lo = y_up(from_below[:, :half_hidden])
        far_hi = y_down(from_above[:, half_hidden:])
        far = jnp.concatenate((far_lo, far_hi), axis=1)
        kept = jnp.concatenate((hidden, from_above, far, from_below), axis=0)
        away = to_core(kept)

        def down(rows):
            mixed = jnp.dot(rows, down_weight, preferred_element_type=F32)
            return mixed.reshape(4, len(chunk), 16, -1)

        kept, away = down(kept), down(away)
        same = jnp.where(z_hi == core, kept, away)
        cross = jnp.where(z_hi == core, away, kept)
        for k, j in enumerate(chunk):
            straight = along("row", 8, lambda r: (r + 2 * j) % 8)
            turned = along("row", 8, lambda r: ((r + 2 * j) % 8) ^ 1)
            here = same[:, k].reshape(64, -1)
            arrived.append(here if j == 0 else straight(here.astype(BF16)).astype(F32))
            arrived.append(turned(cross[:, k].reshape(64, -1).astype(BF16)).astype(F32))

    out = sum(arrived).astype(BF16)
    doubled = jnp.concatenate((out, out), axis=0)
    return lax.dynamic_slice_in_dim(doubled, 64 - y * 16, 64, 0)


def solution(mesh):
    placed = (P(("row", "col"), None), P("col", "row"), P("col", "row"), P("row", "col"))
    return jax.shard_map(
        per_device, mesh=mesh, in_specs=placed, out_specs=P("row", "col"), check_vma=False
    )
```

```python
import jax
import jax.numpy as jnp
from jax import lax
from jax.experimental import pallas as pl
from jax.experimental.pallas import tpu as pltpu
from jax.sharding import Mesh, PartitionSpec as P

F32, BF16, F16 = jnp.float32, jnp.bfloat16, jnp.float16
LIFT = 8.0
TILE = 256
AXES = ("x", "z_hi", "y", "z_lo", "core")
CHUNKS = ((0,), (1,), (3,), (2,))
ORDER = (
    (1, -1), (0, 0), (2, -1), (3, -1), (0, 2), (1, 0), (2, 0), (1, 2), (0, 3), (2, 2), (3, 0),
    (1, 3), (0, 4), (3, 2), (2, 3), (0, 5), (1, 4), (3, 3), (2, 4), (0, 6), (1, 5), (3, 4),
    (2, 5), (1, 6), (0, 7), (2, 6), (3, 5), (0, 8), (1, 7), (3, 6), (2, 7), (1, 8), (3, 7),
    (2, 8), (3, 8),
)


def permute(axes, sizes, move):
    def flat(place):
        index = 0
        for size, part in zip(sizes, place):
            index = index * size + part % size
        return index

    places = [()]
    for size in sizes:
        places = [p + (i,) for p in places for i in range(size)]
    pairs = [(flat(p), flat(move(*p))) for p in places]
    return lambda v: lax.ppermute(v, axes, pairs)


def lifted(v):
    return (v * LIFT).astype(F16)


def lowered(v):
    return v.astype(F32) * (1 / LIFT)


def multiply(rows, *refs):
    half = len(refs) // 2
    for weight, out in zip(refs[:half], refs[half:]):

        @pl.loop(0, weight.shape[1] // TILE)
        def _(i):
            columns = pl.ds(pl.multiple_of(i * TILE, TILE), TILE)
            out[:, columns] = jnp.dot(rows[...], weight[:, columns], preferred_element_type=F32)


def product(rows, *weights):
    vmem = pl.BlockSpec(memory_space=pltpu.VMEM)
    return pl.pallas_call(
        multiply,
        out_shape=[jax.ShapeDtypeStruct((rows.shape[0], w.shape[1]), F32) for w in weights],
        in_specs=[vmem] * (1 + len(weights)),
        out_specs=[vmem] * len(weights),
        compiler_params=pltpu.CompilerParams(vmem_limit_bytes=48 * 2**20),
        cost_estimate=pl.CostEstimate(flops=0, bytes_accessed=0, transcendentals=0),
    )(rows, *weights)


def per_device(tokens, gate_weight, up_weight, down_weight):
    z_hi, y, core = (lax.axis_index(a) for a in ("z_hi", "y", "core"))
    swap_core = permute(("core",), (2,), lambda c: (1 - c,))
    swap_z = permute(("z_lo",), (2,), lambda z: (1 - z,))
    swap_first = permute(("y", "core"), (4, 2), lambda y, c: (y ^ (3 if c else 1), c))
    swap_second = permute(("y", "core"), (4, 2), lambda y, c: (y ^ (1 if c else 3), c))
    along_x = {j: permute(("x",), (4,), lambda x, j=j: (x + j,)) for j in (1, 2, 3)}
    along_row = {
        (j, t): permute(("x", "z_hi"), (4, 2), lambda x, z, j=j, t=t: (x + j, z ^ t))
        for j in range(4)
        for t in range(2)
    }

    features = tokens.shape[1] // 16
    blocks = tokens.reshape(4, 16, features).transpose(1, 0, 2).reshape(1, 64, features)
    blocks = jnp.broadcast_to(blocks, (2, 64, features)).reshape(128, features)
    mine = lax.all_to_all(blocks, AXES[1:], split_axis=0, concat_axis=0, tiled=True)
    mine = mine.reshape(2, 4, 16, features)

    def ordered(half):
        own = lax.dynamic_index_in_dim(mine, half, 0, keepdims=False)
        first = jnp.where(half == 0, 1, 3)
        places = (y, y ^ (4 - first), y ^ first, y ^ 2)
        return [lax.dynamic_index_in_dim(own, p, 0, keepdims=False) for p in places]

    own = jnp.stack(ordered(1 - core) + ordered(core)).reshape(2, 4, 16, features)
    rows = {0: own}

    state = [{} for _ in CHUNKS]
    last = [own]
    arrived = {}

    def tie(*values):
        *values, last[0] = lax.optimization_barrier((*values, last[0]))
        return values

    def step(k, s):
        chunk, st = CHUNKS[k], state[k]
        n = 16 * len(chunk)
        if s == -1:
            for j in chunk:
                rows[j] = along_x[4 - j](*tie(own))
        elif s == 0:
            parts = tie(*[rows[j] for j in chunk])
            both = jnp.stack(parts, axis=2).reshape(8 * n, features)
            terms = product(both, gate_weight, up_weight)
            send = jnp.stack([lifted(v[: 4 * n]) for v in terms])
            send, *st["kept"] = tie(send, *[v[4 * n :] for v in terms])
            st["flight"] = swap_core(send)
        elif s == 2:
            (got,) = tie(st["flight"])
            total = [v + lowered(g) for v, g in zip(st["kept"], got)]
            send = jnp.stack([lifted(v[2 * n :]) for v in total])
            send, *st["kept"] = tie(send, *[v[: 2 * n] for v in total])
            st["flight"] = swap_first(send)
        elif s == 3:
            (got,) = tie(st["flight"])
            total = [v + lowered(g) for v, g in zip(st["kept"], got)]
            send = jnp.stack([lifted(v[n:]) for v in total])
            send, *st["kept"] = tie(send, *[v[:n] for v in total])
            st["flight"] = swap_second(send)
        elif s == 4:
            (got,) = tie(st["flight"])
            total = [v + lowered(g) for v, g in zip(st["kept"], got)]
            send, *st["kept"] = tie(jnp.stack([lifted(v) for v in total]), *total)
            st["flight"] = swap_z(send)
        elif s == 5:
            (got,) = tie(st["flight"])
            gate, up = [v + lowered(g) for v, g in zip(st["kept"], got)]
            (st["hidden"],) = tie((jax.nn.silu(gate) * up).astype(BF16))
            st["flight"] = swap_second(st["hidden"])
        elif s == 6:
            (got,) = tie(st["flight"])
            (st["hidden"],) = tie(jnp.concatenate((st["hidden"], got)))
            st["flight"] = swap_first(st["hidden"])
        elif s == 7:
            (got,) = tie(st["flight"])
            (st["hidden"],) = tie(jnp.concatenate((st["hidden"], got)))
            st["flight"] = swap_core(st["hidden"])
        elif s == 8:
            (got,) = tie(st["flight"])
            both = jnp.concatenate((got, st["hidden"]))
            (mixed,) = product(both, down_weight)
            mixed = mixed.reshape(2, 4, len(chunk), 16, -1)
            stays = z_hi == core
            same = jnp.where(stays, mixed[1], mixed[0])
            cross = jnp.where(stays, mixed[0], mixed[1])
            sends = []
            for i, j in enumerate(chunk):
                here = same[:, i].reshape(64, -1)
                sends.append(here if j == 0 else here.astype(BF16))
                sends.append(cross[:, i].reshape(64, -1).astype(BF16))
            sends = tie(*sends)
            for i, j in enumerate(chunk):
                here, there = sends[2 * i : 2 * i + 2]
                arrived[j, 0] = here if j == 0 else along_row[j, 0](here).astype(F32)
                arrived[j, 1] = along_row[j, 1](there).astype(F32)

    for k, s in ORDER:
        step(k, s)

    out = sum(arrived.values()).astype(BF16).reshape(4, 16, -1)
    first = jnp.where(z_hi == 0, 1, 3)
    where = jnp.stack([jnp.where(e == 0, 0, jnp.where(e == 2, 3, jnp.where(e == first, 2, 1))) for e in range(4)])
    blocks = [lax.dynamic_index_in_dim(out, where[y ^ p], 0, keepdims=False) for p in range(4)]
    return jnp.concatenate(blocks)


def solution(mesh):
    grid = Mesh(mesh.devices.reshape(4, 2, 4, 2, 2), AXES)
    row, col = AXES[:2], AXES[2:]
    placed = (P(AXES, None), P(col, row), P(col, row), P(row, col))
    return jax.shard_map(
        per_device, mesh=grid, in_specs=placed, out_specs=P(row, col), check_vma=False
    )
```

```python
import jax
import jax.numpy as jnp
from jax import lax
from jax.experimental import pallas as pl
from jax.experimental.pallas import tpu as pltpu
from jax.sharding import Mesh, PartitionSpec as P

F32, BF16, F16 = jnp.float32, jnp.bfloat16, jnp.float16
LIFT = 8.0
AXES = ("x", "z_hi", "y", "z_lo", "core")
CHUNKS = ((0,), (1,), (2,), (3,))
ORDER = (
    (1, -1), (2, -1), (0, 0), (3, -1), (0, 2), (1, 0), (1, 2), (2, 0), (0, 3), (2, 2), (1, 3),
    (0, 4), (3, 0), (2, 3), (1, 4), (3, 2), (0, 5), (2, 4), (1, 5), (3, 3), (0, 6), (2, 5),
    (1, 6), (3, 4), (0, 7), (2, 6), (0, 8), (1, 7), (3, 5), (1, 8), (2, 7), (3, 6), (2, 8),
    (3, 7), (3, 8),
)


def permute(axes, sizes, move):
    def flat(place):
        index = 0
        for size, part in zip(sizes, place):
            index = index * size + part % size
        return index

    places = [()]
    for size in sizes:
        places = [p + (i,) for p in places for i in range(size)]
    pairs = [(flat(p), flat(move(*p))) for p in places]
    return lambda v: lax.ppermute(v, axes, pairs)


def lifted(v):
    return (v * LIFT).astype(F16)


def lowered(v):
    return v.astype(F32) * (1 / LIFT)


def copy_in(*refs):
    half = (len(refs) - 1) // 2
    sems = refs[-1]
    copies = [
        pltpu.make_async_copy(here, there, sems.at[i])
        for i, (here, there) in enumerate(zip(refs[:half], refs[half : 2 * half]))
    ]
    for copy in copies:
        copy.start()
    for copy in copies:
        copy.wait()


def held(*weights):
    return pl.pallas_call(
        copy_in,
        out_shape=[pltpu.VMEM(w.shape, w.dtype) for w in weights],
        in_specs=[pl.BlockSpec(memory_space=pltpu.HBM)] * len(weights),
        out_specs=[pl.BlockSpec(memory_space=pltpu.VMEM)] * len(weights),
        scratch_shapes=[pltpu.SemaphoreType.DMA((len(weights),))],
        compiler_params=pltpu.CompilerParams(vmem_limit_bytes=2**20),
        cost_estimate=pl.CostEstimate(
            flops=0, bytes_accessed=sum(2 * w.size for w in weights), transcendentals=0
        ),
    )(*weights)


def product(rows, *weights):
    return [jnp.dot(rows, w, preferred_element_type=F32) for w in weights]


def per_device(tokens, gate_weight, up_weight, down_weight):
    z_hi, y, core = (lax.axis_index(a) for a in ("z_hi", "y", "core"))
    swap_core = permute(("core",), (2,), lambda c: (1 - c,))
    swap_z = permute(("z_lo",), (2,), lambda z: (1 - z,))
    swap_first = permute(("y", "core"), (4, 2), lambda y, c: (y ^ (3 if c else 1), c))
    swap_second = permute(("y", "core"), (4, 2), lambda y, c: (y ^ (1 if c else 3), c))
    along_x = {j: permute(("x",), (4,), lambda x, j=j: (x + j,)) for j in (1, 2, 3)}
    along_row = {
        (j, t): permute(("x", "z_hi"), (4, 2), lambda x, z, j=j, t=t: (x + j, z ^ t))
        for j in range(4)
        for t in range(2)
    }

    features = tokens.shape[1] // 16
    blocks = tokens.reshape(4, 16, features).transpose(1, 0, 2).reshape(1, 64, features)
    blocks = jnp.broadcast_to(blocks, (2, 64, features)).reshape(128, features)
    blocks, *weights = lax.optimization_barrier((blocks, gate_weight, up_weight, down_weight))
    mine = lax.all_to_all(blocks, AXES[1:], split_axis=0, concat_axis=0, tiled=True)
    mine, gate_weight, up_weight, down_weight = lax.optimization_barrier((mine, *held(*weights)))
    mine = mine.reshape(2, 4, 16, features)

    def ordered(half):
        own = lax.dynamic_index_in_dim(mine, half, 0, keepdims=False)
        first = jnp.where(half == 0, 1, 3)
        places = (y, y ^ (4 - first), y ^ first, y ^ 2)
        return [lax.dynamic_index_in_dim(own, p, 0, keepdims=False) for p in places]

    own = jnp.stack(ordered(1 - core) + ordered(core)).reshape(2, 4, 16, features)
    rows = {0: own}

    state = [{} for _ in CHUNKS]
    last = [own]
    arrived = {}

    def tie(*values):
        *values, last[0] = lax.optimization_barrier((*values, last[0]))
        return values

    def step(k, s):
        chunk, st = CHUNKS[k], state[k]
        n = 16 * len(chunk)
        if s == -1:
            for j in chunk:
                rows[j] = along_x[4 - j](*tie(own))
        elif s == 0:
            parts = tie(*[rows[j] for j in chunk])
            both = jnp.stack(parts, axis=2).reshape(8 * n, features)
            terms = product(both, gate_weight, up_weight)
            send = jnp.stack([lifted(v[: 4 * n]) for v in terms])
            send, *st["kept"] = tie(send, *[v[4 * n :] for v in terms])
            st["flight"] = swap_core(send)
        elif s == 2:
            (got,) = tie(st["flight"])
            total = [v + lowered(g) for v, g in zip(st["kept"], got)]
            send = jnp.stack([lifted(v[2 * n :]) for v in total])
            send, *st["kept"] = tie(send, *[v[: 2 * n] for v in total])
            st["flight"] = swap_first(send)
        elif s == 3:
            (got,) = tie(st["flight"])
            total = [v + lowered(g) for v, g in zip(st["kept"], got)]
            send = jnp.stack([lifted(v[n:]) for v in total])
            send, *st["kept"] = tie(send, *[v[:n] for v in total])
            st["flight"] = swap_second(send)
        elif s == 4:
            (got,) = tie(st["flight"])
            total = [v + lowered(g) for v, g in zip(st["kept"], got)]
            send, *st["kept"] = tie(jnp.stack([lifted(v) for v in total]), *total)
            st["flight"] = swap_z(send)
        elif s == 5:
            (got,) = tie(st["flight"])
            gate, up = [v + lowered(g) for v, g in zip(st["kept"], got)]
            (st["hidden"],) = tie((jax.nn.silu(gate) * up).astype(BF16))
            st["flight"] = swap_second(st["hidden"])
        elif s == 6:
            (got,) = tie(st["flight"])
            (st["hidden"],) = tie(jnp.concatenate((st["hidden"], got)))
            st["flight"] = swap_first(st["hidden"])
        elif s == 7:
            (got,) = tie(st["flight"])
            (st["hidden"],) = tie(jnp.concatenate((st["hidden"], got)))
            st["flight"] = swap_core(st["hidden"])
        elif s == 8:
            (got,) = tie(st["flight"])
            both = jnp.concatenate((got, st["hidden"]))
            (mixed,) = product(both, down_weight)
            mixed = mixed.reshape(2, 4, len(chunk), 16, -1)
            stays = z_hi == core
            same = jnp.where(stays, mixed[1], mixed[0])
            cross = jnp.where(stays, mixed[0], mixed[1])
            sends = []
            for i, j in enumerate(chunk):
                here = same[:, i].reshape(64, -1)
                sends.append(here if j == 0 else here.astype(BF16))
                sends.append(cross[:, i].reshape(64, -1).astype(BF16))
            sends = tie(*sends)
            for i, j in enumerate(chunk):
                here, there = sends[2 * i : 2 * i + 2]
                arrived[j, 0] = here if j == 0 else along_row[j, 0](here).astype(F32)
                arrived[j, 1] = along_row[j, 1](there).astype(F32)

    for k, s in ORDER:
        step(k, s)

    out = sum(arrived.values()).astype(BF16).reshape(4, 16, -1)
    first = jnp.where(z_hi == 0, 1, 3)
    where = jnp.stack([jnp.where(e == 0, 0, jnp.where(e == 2, 3, jnp.where(e == first, 2, 1))) for e in range(4)])
    blocks = [lax.dynamic_index_in_dim(out, where[y ^ p], 0, keepdims=False) for p in range(4)]
    return jnp.concatenate(blocks)


def solution(mesh):
    grid = Mesh(mesh.devices.reshape(4, 2, 4, 2, 2), AXES)
    row, col = AXES[:2], AXES[2:]
    placed = (P(AXES, None), P(col, row), P(col, row), P(row, col))
    return jax.shard_map(
        per_device, mesh=grid, in_specs=placed, out_specs=P(row, col), check_vma=False
    )
```

```python
import jax
import jax.numpy as jnp
from jax import lax
from jax.sharding import Mesh, PartitionSpec as P

F32, BF16, F16 = jnp.float32, jnp.bfloat16, jnp.float16
LIFT = 8.0
AXES = ("x", "z_hi", "y", "z_lo", "core")


def permute(axes, sizes, move):
    def flat(place):
        index = 0
        for size, part in zip(sizes, place):
            index = index * size + part
        return index

    places = [()]
    for size in sizes:
        places = [p + (i,) for p in places for i in range(size)]
    pairs = [(flat(p), flat(move(*p))) for p in places]
    return lambda v: lax.ppermute(v, axes, pairs)


def lifted(v):
    return (v * LIFT).astype(F16)


def lowered(v):
    return v.astype(F32) * (1 / LIFT)


def per_device(tokens, gate_weight, up_weight, down_weight):
    z_hi, y, core = (lax.axis_index(a) for a in ("z_hi", "y", "core"))
    swap_core = permute(("core",), (2,), lambda c: (c ^ 1,))
    swap_z = permute(("z_lo",), (2,), lambda z: (z ^ 1,))
    swap_first = permute(("y", "core"), (4, 2), lambda y, c: (y ^ (3 if c else 1), c))
    swap_second = permute(("y", "core"), (4, 2), lambda y, c: (y ^ (1 if c else 3), c))
    swap_x = {e: permute(("x",), (4,), lambda x, e=e: (x ^ e,)) for e in (1, 2, 3)}
    swap_row = {
        e: permute(("x", "z_hi"), (4, 2), lambda x, z, e=e: (x ^ e, z ^ 1)) for e in range(4)
    }

    features = tokens.shape[1] // 16
    blocks = tokens.reshape(4, 16, features).transpose(1, 0, 2).reshape(1, 64, features)
    blocks = jnp.broadcast_to(blocks, (2, 64, features)).reshape(128, features)
    mine = lax.all_to_all(blocks, AXES[1:], split_axis=0, concat_axis=0, tiled=True)
    mine = mine.reshape(2, 4, 16, features)

    def places(half):
        first = jnp.where(half == 0, 1, 3)
        return (y, y ^ (4 - first), y ^ first, y ^ 2)

    halves = (1 - core, core)
    own = jnp.concatenate(
        [
            lax.dynamic_slice(mine, (half, p, 0, 0), (1, 1, 16, features)).reshape(16, features)
            for half in halves
            for p in places(half)
        ]
    )
    rows = {0: own}
    state = [{} for _ in range(4)]
    arrived = []
    stays = z_hi == core

    def tie(*values):
        values = lax.optimization_barrier(values)
        return values if len(values) > 1 else values[0]

    def product(rows, weight):
        return jnp.dot(rows, weight, preferred_element_type=F32)

    def parted(mixed):
        away, kept = mixed[:64], mixed[64:]
        return jnp.where(stays, kept, away), jnp.where(stays, away, kept)

    def step(e, s):
        st = state[e]
        if s == -1:
            rows[e] = swap_x[e](tie(own))
        elif s == 0:
            both = tie(rows[e])
            terms = [product(both, w) for w in (gate_weight, up_weight)]
            send, *st["total"] = tie(jnp.stack([lifted(v[:64]) for v in terms]), *terms)
            st["flight"] = swap_core(send)
        elif s in (2, 3, 4):
            got = tie(st["flight"])
            part = slice(64, 128) if s == 2 else slice(0, got.shape[1])
            total = [v[part] + lowered(g) for v, g in zip(st["total"], got)]
            part = slice(0 if s == 4 else got.shape[1] // 2, None)
            send, *st["total"] = tie(jnp.stack([lifted(v[part]) for v in total]), *total)
            st["flight"] = (swap_first, swap_second, swap_z)[s - 2](send)
        elif s == 5:
            gate, up = [v + lowered(g) for v, g in zip(st["total"], tie(st["flight"]))]
            st["hidden"] = tie((jax.nn.silu(gate) * up).astype(BF16))
            st["flight"] = swap_second(st["hidden"])
        elif s in (6, 7):
            st["hidden"] = tie(jnp.concatenate((st["hidden"], tie(st["flight"]))))
            st["flight"] = (swap_first if s == 6 else swap_core)(st["hidden"])
        elif s == 8:
            both = jnp.concatenate((tie(st["flight"]), st["hidden"]))
            mixed = product(both, down_weight)
            same, cross = parted(mixed)
            if e == 0:
                same, cross = tie(same, cross.astype(BF16))
                arrived.append(same)
            else:
                same, cross = tie(same.astype(BF16), cross.astype(BF16))
                arrived.append(swap_x[e](same).astype(F32))
            arrived.append(swap_row[e](cross).astype(F32))

    for s in (-1, 0, 2, 3, 4, 5, 6, 7, 8):
        for e in (0, 2, 1, 3):
            if e or s >= 0:
                step(e, s)

    out = sum(arrived).astype(BF16).reshape(4, 16, -1)
    first = jnp.where(z_hi == 0, 1, 3)
    blocks = []
    for p in range(4):
        e = y ^ p
        place = jnp.where(e == 0, 0, jnp.where(e == 2, 3, jnp.where(e == first, 2, 1)))
        blocks.append(lax.dynamic_index_in_dim(out, place, 0, keepdims=False))
    return jnp.concatenate(blocks)


def solution(mesh):
    grid = Mesh(mesh.devices.reshape(4, 2, 4, 2, 2), AXES)
    row, col = AXES[:2], AXES[2:]
    placed = (P(AXES, None), P(col, row), P(col, row), P(row, col))
    return jax.shard_map(
        per_device, mesh=grid, in_specs=placed, out_specs=P(row, col), check_vma=False
    )
```

```python
import jax
import jax.numpy as jnp
from jax import lax
from jax.sharding import Mesh, PartitionSpec as P

F32, BF16, F16 = jnp.float32, jnp.bfloat16, jnp.float16
LIFT = 8.0
AXES = ("x", "z_hi", "y", "z_lo", "core")
ORDER = (
    *((e, -1) for e in (1, 3, 2)),
    *((e, s) for s in (0, 2, 3) for e in (0, 1)),
    *((e, s) for s in (0, 2) for e in (2, 3)),
    *((e, 4) for e in (0, 1)),
    *((e, 3) for e in (2, 3)),
    *((e, 5) for e in (0, 1)),
    *((e, 4) for e in (2, 3)),
    *((e, 6) for e in (0, 1)),
    *((e, 5) for e in (2, 3)),
    *((e, 7) for e in (0, 1)),
    *((e, 6) for e in (2, 3)),
    *((e, 8) for e in (0, 1)),
    *((e, s) for s in (7, 8) for e in (2, 3)),
)


def permute(axes, sizes, move):
    def flat(place):
        index = 0
        for size, part in zip(sizes, place):
            index = index * size + part
        return index

    places = [()]
    for size in sizes:
        places = [p + (i,) for p in places for i in range(size)]
    pairs = [(flat(p), flat(move(*p))) for p in places]
    return lambda v: lax.ppermute(v, axes, pairs)


def lifted(v):
    return (v * LIFT).astype(F16)


def lowered(v):
    return v.astype(F32) * (1 / LIFT)


def per_device(tokens, gate_weight, up_weight, down_weight):
    z_hi, y, core = (lax.axis_index(a) for a in ("z_hi", "y", "core"))
    swap_core = permute(("core",), (2,), lambda c: (c ^ 1,))
    swap_z = permute(("z_lo",), (2,), lambda z: (z ^ 1,))
    swap_first = permute(("y", "core"), (4, 2), lambda y, c: (y ^ (3 if c else 1), c))
    swap_second = permute(("y", "core"), (4, 2), lambda y, c: (y ^ (1 if c else 3), c))
    swap_x = {e: permute(("x",), (4,), lambda x, e=e: (x ^ e,)) for e in (1, 2, 3)}
    swap_z_hi = permute(("z_hi",), (2,), lambda z: (z ^ 1,))

    features = tokens.shape[1] // 16
    blocks = tokens.reshape(4, 16, features).transpose(1, 0, 2).reshape(1, 64, features)
    blocks = jnp.broadcast_to(blocks, (2, 64, features)).reshape(128, features)
    mine = lax.all_to_all(blocks, AXES[1:], split_axis=0, concat_axis=0, tiled=True)
    mine = mine.reshape(2, 4, 16, features)

    def places(half):
        first = jnp.where(half == 0, 1, 3)
        return (y, y ^ (4 - first), y ^ first, y ^ 2)

    halves = (1 - core, core)
    own = jnp.concatenate(
        [
            lax.dynamic_slice(mine, (half, p, 0, 0), (1, 1, 16, features)).reshape(16, features)
            for half in halves
            for p in places(half)
        ]
    )
    rows = {0: own}
    state = [{} for _ in range(4)]
    arrived = []
    stays = z_hi == core

    def tie(*values):
        values = lax.optimization_barrier(values)
        return values if len(values) > 1 else values[0]

    def product(rows, weight):
        return jnp.dot(rows, weight, preferred_element_type=F32)

    def parted(mixed):
        away, kept = mixed[:64], mixed[64:]
        return jnp.where(stays, kept, away), jnp.where(stays, away, kept)

    def step(e, s):
        st = state[e]
        if s == -1:
            rows[e] = swap_x[e](tie(own))
        elif s == 0:
            both = rows[e]
            if e > 1:
                both, _ = tie(both, state[e - 2]["send", 3])
            terms = [product(both, w) for w in (gate_weight, up_weight)]
            send, *st["total"] = tie(jnp.stack([lifted(v[:64]) for v in terms]), *terms)
            st["flight"] = swap_core(send)
        elif s in (2, 3, 4):
            got = tie(st["flight"])
            if s == 4 and e < 2:
                got, _ = tie(got, state[e + 2]["send", 2])
            part = slice(64, 128) if s == 2 else slice(0, got.shape[1])
            total = [v[part] + lowered(g) for v, g in zip(st["total"], got)]
            part = slice(0 if s == 4 else got.shape[1] // 2, None)
            send, *st["total"] = tie(jnp.stack([lifted(v[part]) for v in total]), *total)
            st["send", s] = send
            st["flight"] = (swap_first, swap_second, swap_z)[s - 2](send)
        elif s == 5:
            gate, up = [v + lowered(g) for v, g in zip(st["total"], tie(st["flight"]))]
            st["hidden"] = tie((jax.nn.silu(gate) * up).astype(BF16))
            st["flight"] = swap_second(st["hidden"])
        elif s in (6, 7):
            st["hidden"] = tie(jnp.concatenate((st["hidden"], tie(st["flight"]))))
            st["flight"] = (swap_first if s == 6 else swap_core)(st["hidden"])
        elif s == 8:
            both = jnp.concatenate((tie(st["flight"]), st["hidden"]))
            mixed = product(both, down_weight)
            if e == 0:
                arrived.append(tie(mixed))
            else:
                arrived.append(swap_x[e](tie(mixed.astype(BF16))).astype(F32))

    for e, s in ORDER:
        step(e, s)
    same, cross = parted(sum(arrived))
    same, cross = tie(same, cross.astype(BF16))

    out = (same + swap_z_hi(cross).astype(F32)).astype(BF16).reshape(4, 16, -1)
    first = jnp.where(z_hi == 0, 1, 3)
    blocks = []
    for p in range(4):
        e = y ^ p
        place = jnp.where(e == 0, 0, jnp.where(e == 2, 3, jnp.where(e == first, 2, 1)))
        blocks.append(lax.dynamic_index_in_dim(out, place, 0, keepdims=False))
    return jnp.concatenate(blocks)


def solution(mesh):
    grid = Mesh(mesh.devices.reshape(4, 2, 4, 2, 2), AXES)
    row, col = AXES[:2], AXES[2:]
    placed = (P(AXES, None), P(col, row), P(col, row), P(row, col))
    return jax.shard_map(
        per_device, mesh=grid, in_specs=placed, out_specs=P(row, col), check_vma=False
    )
```

```python
import jax
import jax.numpy as jnp
from jax import lax
from jax.sharding import Mesh, PartitionSpec as P

F32, BF16, F16 = jnp.float32, jnp.bfloat16, jnp.float16
LIFT = 8.0
AXES = ("x", "z_hi", "y", "z_lo", "core")
Z_FIRST = 0


def permute(axes, sizes, move):
    def flat(place):
        index = 0
        for size, part in zip(sizes, place):
            index = index * size + part
        return index

    places = [()]
    for size in sizes:
        places = [p + (i,) for p in places for i in range(size)]
    pairs = [(flat(p), flat(move(*p))) for p in places]
    return lambda v: lax.ppermute(v, axes, pairs)


def lifted(v):
    return (v * LIFT).astype(F16)


def lowered(v):
    return v.astype(F32) * (1 / LIFT)


def per_device(tokens, gate_weight, up_weight, down_weight):
    z_hi, y, z_lo, core = (lax.axis_index(a) for a in AXES[1:])
    swap_core = permute(("core",), (2,), lambda c: (c ^ 1,))
    swap_z = permute(("z_lo",), (2,), lambda z: (z ^ 1,))
    swap_first = permute(("y", "core"), (4, 2), lambda y, c: (y ^ (3 if c else 1), c))
    swap_second = permute(("y", "core"), (4, 2), lambda y, c: (y ^ (1 if c else 3), c))
    swap_x = {e: permute(("x",), (4,), lambda x, e=e: (x ^ e,)) for e in (1, 2, 3)}
    swap_row = {
        e: permute(("x", "z_hi"), (4, 2), lambda x, z, e=e: (x ^ e, z ^ 1)) for e in range(4)
    }

    features = tokens.shape[1] // 16
    blocks = tokens.reshape(4, 16, features).transpose(1, 0, 2).reshape(1, 64, features)
    blocks = jnp.broadcast_to(blocks, (2, 64, features)).reshape(128, features)
    mine = lax.all_to_all(blocks, AXES[1:], split_axis=0, concat_axis=0, tiled=True)
    mine = mine.reshape(2, 4, 16, features)

    def places(half):
        first = jnp.where(half == 0, 1, 3)
        return (y, y ^ (4 - first), y ^ first, y ^ 2)

    halves = (1 - core, core)
    own = jnp.concatenate(
        [
            lax.dynamic_slice(mine, (half, p, 0, 0), (1, 1, 16, features)).reshape(16, features)
            for half in halves
            for p in places(half)
        ]
    )
    rows = {0: own}
    state = [{} for _ in range(4)]
    arrived = []
    half_hidden = gate_weight.shape[1] // 2
    stays = z_hi == core

    def tie(*values):
        values = lax.optimization_barrier(values)
        return values if len(values) > 1 else values[0]

    def product(rows, weight):
        return jnp.dot(rows, weight, preferred_element_type=F32)

    def parted(mixed):
        away, kept = mixed[:64], mixed[64:]
        return jnp.where(stays, kept, away), jnp.where(stays, away, kept)

    def step(e, s):
        st = state[e]
        if s == -1:
            rows[e] = swap_x[e](tie(own))
        elif s == 0:
            both = tie(rows[e])
            terms = [product(both, w) for w in (gate_weight, up_weight)]
            send, *st["total"] = tie(jnp.stack([lifted(v[:64]) for v in terms]), *terms)
            st["flight"] = swap_core(send)
        elif s in (2, 3, 4):
            got = tie(st["flight"])
            part = slice(64, 128) if s == 2 else slice(0, got.shape[1])
            total = [v[part] + lowered(g) for v, g in zip(st["total"], got)]
            if e == Z_FIRST and s == 2:
                sides = [(v[:, :half_hidden], v[:, half_hidden:]) for v in total]
                send = jnp.stack([lifted(jnp.where(z_lo == 0, hi, lo)) for lo, hi in sides])
                total = [jnp.where(z_lo == 0, lo, hi) for lo, hi in sides]
                swap = swap_z
            else:
                over = s - 1 if e == Z_FIRST else s
                part = slice(0 if over == 4 else got.shape[1] // 2, None)
                send = jnp.stack([lifted(v[part]) for v in total])
                swap = (swap_first, swap_second, swap_z)[over - 2]
            send, *st["total"] = tie(send, *total)
            st["flight"] = swap(send)
        elif s == 5:
            got = tie(st["flight"])
            gate, up = [v[: got.shape[1]] + lowered(g) for v, g in zip(st["total"], got)]
            st["hidden"] = tie((jax.nn.silu(gate) * up).astype(BF16))
            if e == Z_FIRST:
                near, far = st["hidden"], tie(swap_z(st["hidden"]))
                sides = (jnp.where(z_lo == 0, near, far), jnp.where(z_lo == 0, far, near))
                st["hidden"] = tie(jnp.concatenate(sides, axis=1))
            st["flight"] = swap_second(st["hidden"])
        elif s in (6, 7):
            st["hidden"] = tie(jnp.concatenate((st["hidden"], tie(st["flight"]))))
            st["flight"] = (swap_first if s == 6 else swap_core)(st["hidden"])
        elif s == 8:
            both = jnp.concatenate((tie(st["flight"]), st["hidden"]))
            mixed = product(both, down_weight)
            same, cross = parted(mixed)
            if e == 0:
                same, cross = tie(same, cross.astype(BF16))
                arrived.append(same)
            else:
                same, cross = tie(same.astype(BF16), cross.astype(BF16))
                arrived.append(swap_x[e](same).astype(F32))
            arrived.append(swap_row[e](cross).astype(F32))

    for s in (-1, 0, 2, 3, 4, 5, 6, 7, 8):
        for e in (0, 2, 1, 3):
            if e or s >= 0:
                step(e, s)

    out = sum(arrived).astype(BF16).reshape(4, 16, -1)
    first = jnp.where(z_hi == 0, 1, 3)
    blocks = []
    for p in range(4):
        e = y ^ p
        place = jnp.where(e == 0, 0, jnp.where(e == 2, 3, jnp.where(e == first, 2, 1)))
        blocks.append(lax.dynamic_index_in_dim(out, place, 0, keepdims=False))
    return jnp.concatenate(blocks)


def solution(mesh):
    grid = Mesh(mesh.devices.reshape(4, 2, 4, 2, 2), AXES)
    row, col = AXES[:2], AXES[2:]
    placed = (P(AXES, None), P(col, row), P(col, row), P(row, col))
    return jax.shard_map(
        per_device, mesh=grid, in_specs=placed, out_specs=P(row, col), check_vma=False
    )
```

```python
import jax
import jax.numpy as jnp
from jax import lax
from jax.sharding import Mesh, PartitionSpec as P

F32, BF16, F16 = jnp.float32, jnp.bfloat16, jnp.float16
LIFT = 8.0
AXES = ("x", "z_hi", "y", "z_lo", "core")
Z_FIRST = 3


def permute(axes, sizes, move):
    def flat(place):
        index = 0
        for size, part in zip(sizes, place):
            index = index * size + part
        return index

    places = [()]
    for size in sizes:
        places = [p + (i,) for p in places for i in range(size)]
    pairs = [(flat(p), flat(move(*p))) for p in places]
    return lambda v: lax.ppermute(v, axes, pairs)


def lifted(v):
    return (v * LIFT).astype(F16)


def lowered(v):
    return v.astype(F32) * (1 / LIFT)


def per_device(tokens, gate_weight, up_weight, down_weight):
    z_hi, y, z_lo, core = (lax.axis_index(a) for a in AXES[1:])
    swap_core = permute(("core",), (2,), lambda c: (c ^ 1,))
    swap_z = permute(("z_lo",), (2,), lambda z: (z ^ 1,))
    swap_first = permute(("y", "core"), (4, 2), lambda y, c: (y ^ (3 if c else 1), c))
    swap_second = permute(("y", "core"), (4, 2), lambda y, c: (y ^ (1 if c else 3), c))
    swap_x = {e: permute(("x",), (4,), lambda x, e=e: (x ^ e,)) for e in (1, 2, 3)}
    swap_row = {
        e: permute(("x", "z_hi"), (4, 2), lambda x, z, e=e: (x ^ e, z ^ 1)) for e in range(4)
    }

    features = tokens.shape[1] // 16
    blocks = tokens.reshape(4, 16, features).transpose(1, 0, 2).reshape(1, 64, features)
    blocks = jnp.broadcast_to(blocks, (2, 64, features)).reshape(128, features)
    mine = lax.all_to_all(blocks, AXES[1:], split_axis=0, concat_axis=0, tiled=True)
    mine = mine.reshape(2, 4, 16, features)

    def places(half):
        first = jnp.where(half == 0, 1, 3)
        return (y, y ^ (4 - first), y ^ first, y ^ 2)

    halves = (1 - core, core)
    own = jnp.concatenate(
        [
            lax.dynamic_slice(mine, (half, p, 0, 0), (1, 1, 16, features)).reshape(16, features)
            for half in halves
            for p in places(half)
        ]
    )
    rows = {0: own}
    state = [{} for _ in range(4)]
    arrived = []
    half_hidden = gate_weight.shape[1] // 2
    stays = z_hi == core

    def tie(*values):
        values = lax.optimization_barrier(values)
        return values if len(values) > 1 else values[0]

    def product(rows, weight):
        return jnp.dot(rows, weight, preferred_element_type=F32)

    def parted(mixed):
        away, kept = mixed[:64], mixed[64:]
        return jnp.where(stays, kept, away), jnp.where(stays, away, kept)

    def step(e, s):
        st = state[e]
        if s == -1:
            rows[e] = swap_x[e](tie(own))
        elif s == 0:
            both = tie(rows[e])
            terms = [product(both, w) for w in (gate_weight, up_weight)]
            send, *st["total"] = tie(jnp.stack([lifted(v[:64]) for v in terms]), *terms)
            st["flight"] = swap_core(send)
        elif s in (2, 3, 4):
            got = tie(st["flight"])
            part = slice(64, 128) if s == 2 else slice(0, got.shape[1])
            total = [v[part] + lowered(g) for v, g in zip(st["total"], got)]
            if e == Z_FIRST and s == 2:
                sides = [(v[:, :half_hidden], v[:, half_hidden:]) for v in total]
                send = jnp.stack([lifted(jnp.where(z_lo == 0, hi, lo)) for lo, hi in sides])
                total = [jnp.where(z_lo == 0, lo, hi) for lo, hi in sides]
                swap = swap_z
            else:
                over = s - 1 if e == Z_FIRST else s
                part = slice(0 if over == 4 else got.shape[1] // 2, None)
                send = jnp.stack([lifted(v[part]) for v in total])
                swap = (swap_first, swap_second, swap_z)[over - 2]
            send, *st["total"] = tie(send, *total)
            st["flight"] = swap(send)
        elif s == 5:
            got = tie(st["flight"])
            gate, up = [v[: got.shape[1]] + lowered(g) for v, g in zip(st["total"], got)]
            st["hidden"] = tie((jax.nn.silu(gate) * up).astype(BF16))
            if e == Z_FIRST:
                near, far = st["hidden"], tie(swap_z(st["hidden"]))
                sides = (jnp.where(z_lo == 0, near, far), jnp.where(z_lo == 0, far, near))
                st["hidden"] = tie(jnp.concatenate(sides, axis=1))
            st["flight"] = swap_second(st["hidden"])
        elif s in (6, 7):
            st["hidden"] = tie(jnp.concatenate((st["hidden"], tie(st["flight"]))))
            st["flight"] = (swap_first if s == 6 else swap_core)(st["hidden"])
        elif s == 8:
            both = jnp.concatenate((tie(st["flight"]), st["hidden"]))
            mixed = product(both, down_weight)
            same, cross = parted(mixed)
            if e == 0:
                same, cross = tie(same, cross.astype(BF16))
                arrived.append(same)
            else:
                same, cross = tie(same.astype(BF16), cross.astype(BF16))
                arrived.append(swap_x[e](same).astype(F32))
            arrived.append(swap_row[e](cross).astype(F32))

    for s in (-1, 0, 2, 3, 4, 5, 6, 7, 8):
        for e in (0, 2, 1, 3):
            if e or s >= 0:
                step(e, s)

    out = sum(arrived).astype(BF16).reshape(4, 16, -1)
    first = jnp.where(z_hi == 0, 1, 3)
    blocks = []
    for p in range(4):
        e = y ^ p
        place = jnp.where(e == 0, 0, jnp.where(e == 2, 3, jnp.where(e == first, 2, 1)))
        blocks.append(lax.dynamic_index_in_dim(out, place, 0, keepdims=False))
    return jnp.concatenate(blocks)


def solution(mesh):
    grid = Mesh(mesh.devices.reshape(4, 2, 4, 2, 2), AXES)
    row, col = AXES[:2], AXES[2:]
    placed = (P(AXES, None), P(col, row), P(col, row), P(row, col))
    return jax.shard_map(
        per_device, mesh=grid, in_specs=placed, out_specs=P(row, col), check_vma=False
    )
```

```python
import jax
import jax.numpy as jnp
from jax import lax
from jax.sharding import Mesh, PartitionSpec as P

F32, BF16, F16 = jnp.float32, jnp.bfloat16, jnp.float16
LIFT = 8.0
AXES = ("x", "z_hi", "y", "z_lo", "core")
Z_FIRST = 0


def permute(axes, sizes, move):
    def flat(place):
        index = 0
        for size, part in zip(sizes, place):
            index = index * size + part
        return index

    places = [()]
    for size in sizes:
        places = [p + (i,) for p in places for i in range(size)]
    pairs = [(flat(p), flat(move(*p))) for p in places]
    return lambda v: lax.ppermute(v, axes, pairs)


def lifted(v):
    return (v * LIFT).astype(F16)


def lowered(v):
    return v.astype(F32) * (1 / LIFT)


def per_device(tokens, gate_weight, up_weight, down_weight):
    z_hi, y, z_lo, core = (lax.axis_index(a) for a in AXES[1:])
    swap_core = permute(("core",), (2,), lambda c: (c ^ 1,))
    swap_z = permute(("z_lo",), (2,), lambda z: (z ^ 1,))
    swap_first = permute(("y", "core"), (4, 2), lambda y, c: (y ^ (3 if c else 1), c))
    swap_second = permute(("y", "core"), (4, 2), lambda y, c: (y ^ (1 if c else 3), c))
    swap_x = {e: permute(("x",), (4,), lambda x, e=e: (x ^ e,)) for e in (1, 2, 3)}
    swap_row = {
        e: permute(("x", "z_hi"), (4, 2), lambda x, z, e=e: (x ^ e, z ^ 1)) for e in range(4)
    }

    features = tokens.shape[1] // 16
    blocks = tokens.reshape(4, 16, features).transpose(1, 0, 2)
    mine = lax.all_to_all(blocks, AXES[2:], split_axis=0, concat_axis=0, tiled=True)
    mine = mine.reshape(4, 16, features)

    def places(half):
        first = jnp.where(half == 0, 1, 3)
        return (y, y ^ (4 - first), y ^ first, y ^ 2)

    near = jnp.concatenate(
        [lax.dynamic_index_in_dim(mine, p, 0, keepdims=False) for p in places(z_hi)]
    )
    pairs = {0: (near, swap_row[0](near))}
    for e in (2, 1, 3):
        pairs[e] = (swap_x[e](near), swap_row[e](near))
    stays = z_hi == core
    rows = {
        e: jnp.concatenate((jnp.where(stays, b, a), jnp.where(stays, a, b)))
        for e, (a, b) in pairs.items()
    }
    state = [{} for _ in range(4)]
    half_hidden = gate_weight.shape[1] // 2

    def tie(*values):
        values = lax.optimization_barrier(values)
        return values if len(values) > 1 else values[0]

    def product(rows, weight):
        return jnp.dot(rows, weight, preferred_element_type=F32)

    def parted(mixed):
        away, kept = mixed[:64], mixed[64:]
        return jnp.where(stays, kept, away), jnp.where(stays, away, kept)

    def step(e, s):
        st = state[e]
        if s == 0:
            both = tie(rows[e])
            terms = [product(both, w) for w in (gate_weight, up_weight)]
            send, *st["total"] = tie(jnp.stack([lifted(v[:64]) for v in terms]), *terms)
            st["flight"] = swap_core(send)
        elif s in (2, 3, 4):
            got = tie(st["flight"])
            part = slice(64, 128) if s == 2 else slice(0, got.shape[1])
            total = [v[part] + lowered(g) for v, g in zip(st["total"], got)]
            if e == Z_FIRST and s == 2:
                sides = [(v[:, :half_hidden], v[:, half_hidden:]) for v in total]
                send = jnp.stack([lifted(jnp.where(z_lo == 0, hi, lo)) for lo, hi in sides])
                total = [jnp.where(z_lo == 0, lo, hi) for lo, hi in sides]
                swap = swap_z
            else:
                over = s - 1 if e == Z_FIRST else s
                part = slice(0 if over == 4 else got.shape[1] // 2, None)
                send = jnp.stack([lifted(v[part]) for v in total])
                swap = (swap_first, swap_second, swap_z)[over - 2]
            send, *st["total"] = tie(send, *total)
            st["flight"] = swap(send)
        elif s == 5:
            got = tie(st["flight"])
            gate, up = [v[: got.shape[1]] + lowered(g) for v, g in zip(st["total"], got)]
            st["hidden"] = tie((jax.nn.silu(gate) * up).astype(BF16))
            if e == Z_FIRST:
                near, far = st["hidden"], tie(swap_z(st["hidden"]))
                sides = (jnp.where(z_lo == 0, near, far), jnp.where(z_lo == 0, far, near))
                st["hidden"] = tie(jnp.concatenate(sides, axis=1))
            st["flight"] = swap_second(st["hidden"])
        elif s in (6, 7):
            st["hidden"] = tie(jnp.concatenate((st["hidden"], tie(st["flight"]))))
            st["flight"] = (swap_first if s == 6 else swap_core)(st["hidden"])
        elif s == 8:
            both = jnp.concatenate((tie(st["flight"]), st["hidden"]))
            st["mixed"] = product(both, down_weight)

    for s in (0, 2, 3, 4, 5, 6, 7, 8):
        for e in (0, 2, 1, 3):
            step(e, s)

    mixed = tie(*[st["mixed"] for st in state])
    arrived = []
    for e in (2, 3, 1, 0):
        same, cross = parted(mixed[e])
        if e == 0:
            arrived.append(same)
        else:
            arrived.append(swap_x[e](same.astype(BF16)).astype(F32))
        arrived.append(swap_row[e](cross.astype(BF16)).astype(F32))
    out = sum(arrived).astype(BF16).reshape(4, 16, -1)
    first = jnp.where(z_hi == 0, 1, 3)
    blocks = []
    for p in range(4):
        e = y ^ p
        place = jnp.where(e == 0, 0, jnp.where(e == 2, 3, jnp.where(e == first, 2, 1)))
        blocks.append(lax.dynamic_index_in_dim(out, place, 0, keepdims=False))
    return jnp.concatenate(blocks)


def solution(mesh):
    grid = Mesh(mesh.devices.reshape(4, 2, 4, 2, 2), AXES)
    row, col = AXES[:2], AXES[2:]
    placed = (P(AXES, None), P(col, row), P(col, row), P(row, col))
    return jax.shard_map(
        per_device, mesh=grid, in_specs=placed, out_specs=P(row, col), check_vma=False
    )
```

```python
import jax
import jax.numpy as jnp
from jax import lax
from jax.sharding import Mesh, PartitionSpec as P

F32, BF16, F16 = jnp.float32, jnp.bfloat16, jnp.float16
LIFT = 8.0
AXES = ("x", "z_hi", "y", "z_lo", "core")
Z_FIRST = 3


def permute(axes, sizes, move):
    def flat(place):
        index = 0
        for size, part in zip(sizes, place):
            index = index * size + part
        return index

    places = [()]
    for size in sizes:
        places = [p + (i,) for p in places for i in range(size)]
    pairs = [(flat(p), flat(move(*p))) for p in places]
    return lambda v: lax.ppermute(v, axes, pairs)


def lifted(v):
    return (v * LIFT).astype(F16)


def lowered(v):
    return v.astype(F32) * (1 / LIFT)


def per_device(tokens, gate_weight, up_weight, down_weight):
    z_hi, y, z_lo, core = (lax.axis_index(a) for a in AXES[1:])
    swap_core = permute(("core",), (2,), lambda c: (c ^ 1,))
    swap_z = permute(("z_lo",), (2,), lambda z: (z ^ 1,))
    swap_first = permute(("y", "core"), (4, 2), lambda y, c: (y ^ (3 if c else 1), c))
    swap_second = permute(("y", "core"), (4, 2), lambda y, c: (y ^ (1 if c else 3), c))
    swap_x = {e: permute(("x",), (4,), lambda x, e=e: (x ^ e,)) for e in (1, 2, 3)}
    swap_row = {
        e: permute(("x", "z_hi"), (4, 2), lambda x, z, e=e: (x ^ e, z ^ 1)) for e in range(4)
    }

    features = tokens.shape[1] // 16
    blocks = tokens.reshape(4, 16, features).transpose(1, 0, 2).reshape(1, 64, features)
    blocks = jnp.broadcast_to(blocks, (2, 64, features)).reshape(128, features)
    mine = lax.all_to_all(blocks, AXES[1:], split_axis=0, concat_axis=0, tiled=True)
    mine = mine.reshape(2, 4, 16, features)

    def places(half):
        first = jnp.where(half == 0, 1, 3)
        return (y, y ^ (4 - first), y ^ first, y ^ 2)

    halves = (1 - core, core)
    own = jnp.concatenate(
        [
            lax.dynamic_slice(mine, (half, p, 0, 0), (1, 1, 16, features)).reshape(16, features)
            for half in halves
            for p in places(half)
        ]
    )
    rows = {0: own}
    state = [{} for _ in range(4)]
    arrived = []
    half_hidden = gate_weight.shape[1] // 2
    stays = z_hi == core

    def tie(*values):
        values = lax.optimization_barrier(values)
        return values if len(values) > 1 else values[0]

    def product(rows, weight):
        return jnp.dot(rows, weight, preferred_element_type=F32)

    def parted(mixed):
        away, kept = mixed[:64], mixed[64:]
        return jnp.where(stays, kept, away), jnp.where(stays, away, kept)

    def step(e, s):
        st = state[e]
        if s == -1:
            rows[e] = swap_x[e](tie(own))
        elif s == 0:
            both = tie(rows[e])
            terms = [product(both, w) for w in (gate_weight, up_weight)]
            send, *st["total"] = tie(jnp.stack([lifted(v[:64]) for v in terms]), *terms)
            st["flight"] = swap_core(send)
        elif s in (2, 3, 4):
            got = tie(st["flight"])
            if s == 4 and e == 0:
                got, *_ = tie(got, *[other["send"] for other in state[1:]])
            part = slice(64, 128) if s == 2 else slice(0, got.shape[1])
            total = [v[part] + lowered(g) for v, g in zip(st["total"], got)]
            if e == Z_FIRST and s == 2:
                sides = [(v[:, :half_hidden], v[:, half_hidden:]) for v in total]
                send = jnp.stack([lifted(jnp.where(z_lo == 0, hi, lo)) for lo, hi in sides])
                total = [jnp.where(z_lo == 0, lo, hi) for lo, hi in sides]
                swap = swap_z
            else:
                over = s - 1 if e == Z_FIRST else s
                part = slice(0 if over == 4 else got.shape[1] // 2, None)
                send = jnp.stack([lifted(v[part]) for v in total])
                swap = (swap_first, swap_second, swap_z)[over - 2]
            send, *st["total"] = tie(send, *total)
            st["send"] = send
            st["flight"] = swap(send)
        elif s == 5:
            got = tie(st["flight"])
            gate, up = [v[: got.shape[1]] + lowered(g) for v, g in zip(st["total"], got)]
            st["hidden"] = tie((jax.nn.silu(gate) * up).astype(BF16))
            if e == Z_FIRST:
                near, far = st["hidden"], tie(swap_z(st["hidden"]))
                sides = (jnp.where(z_lo == 0, near, far), jnp.where(z_lo == 0, far, near))
                st["hidden"] = tie(jnp.concatenate(sides, axis=1))
            st["flight"] = swap_second(st["hidden"])
        elif s in (6, 7):
            st["hidden"] = tie(jnp.concatenate((st["hidden"], tie(st["flight"]))))
            st["flight"] = (swap_first if s == 6 else swap_core)(st["hidden"])
        elif s == 8:
            both = jnp.concatenate((tie(st["flight"]), st["hidden"]))
            mixed = product(both, down_weight)
            same, cross = parted(mixed)
            if e == 0:
                same, cross = tie(same, cross.astype(BF16))
                arrived.append(same)
            else:
                same, cross = tie(same.astype(BF16), cross.astype(BF16))
                arrived.append(swap_x[e](same).astype(F32))
            arrived.append(swap_row[e](cross).astype(F32))

    for s in (-1, 0, 2, 3, 4, 5, 6, 7, 8):
        for e in range(4):
            if e or s >= 0:
                step(e, s)

    out = sum(arrived).astype(BF16).reshape(4, 16, -1)
    first = jnp.where(z_hi == 0, 1, 3)
    blocks = []
    for p in range(4):
        e = y ^ p
        place = jnp.where(e == 0, 0, jnp.where(e == 2, 3, jnp.where(e == first, 2, 1)))
        blocks.append(lax.dynamic_index_in_dim(out, place, 0, keepdims=False))
    return jnp.concatenate(blocks)


def solution(mesh):
    grid = Mesh(mesh.devices.reshape(4, 2, 4, 2, 2), AXES)
    row, col = AXES[:2], AXES[2:]
    placed = (P(AXES, None), P(col, row), P(col, row), P(row, col))
    return jax.shard_map(
        per_device, mesh=grid, in_specs=placed, out_specs=P(row, col), check_vma=False
    )
```

```python
import jax
import jax.numpy as jnp
from jax import lax
from jax.sharding import Mesh, PartitionSpec as P

F32, BF16, F16 = jnp.float32, jnp.bfloat16, jnp.float16
LIFT = 8.0
AXES = ("x", "z_hi", "y", "z_lo", "core")
Z_FIRST = 3


def permute(axes, sizes, move):
    def flat(place):
        index = 0
        for size, part in zip(sizes, place):
            index = index * size + part
        return index

    places = [()]
    for size in sizes:
        places = [p + (i,) for p in places for i in range(size)]
    pairs = [(flat(p), flat(move(*p))) for p in places]
    return lambda v: lax.ppermute(v, axes, pairs)


def lifted(v):
    return (v * LIFT).astype(F16)


def lowered(v):
    return v.astype(F32) * (1 / LIFT)


def per_device(tokens, gate_weight, up_weight, down_weight):
    z_hi, y, z_lo, core = (lax.axis_index(a) for a in AXES[1:])
    swap_core = permute(("core",), (2,), lambda c: (c ^ 1,))
    swap_z = permute(("z_lo",), (2,), lambda z: (z ^ 1,))
    swap_first = permute(("y", "core"), (4, 2), lambda y, c: (y ^ (3 if c else 1), c))
    swap_second = permute(("y", "core"), (4, 2), lambda y, c: (y ^ (1 if c else 3), c))
    swap_x = {e: permute(("x",), (4,), lambda x, e=e: (x ^ e,)) for e in (1, 2, 3)}
    swap_row = {
        e: permute(("x", "z_hi"), (4, 2), lambda x, z, e=e: (x ^ e, z ^ 1)) for e in range(3)
    }

    features = tokens.shape[1] // 16
    blocks = tokens.reshape(4, 16, features).transpose(1, 0, 2).reshape(1, 64, features)
    blocks = jnp.broadcast_to(blocks, (2, 64, features)).reshape(128, features)
    mine = lax.all_to_all(blocks, AXES[1:], split_axis=0, concat_axis=0, tiled=True)
    mine = mine.reshape(2, 4, 16, features)

    def places(half):
        first = jnp.where(half == 0, 1, 3)
        return (y, y ^ (4 - first), y ^ first, y ^ 2)

    halves = (1 - core, core)
    own = jnp.concatenate(
        [
            lax.dynamic_slice(mine, (half, p, 0, 0), (1, 1, 16, features)).reshape(16, features)
            for half in halves
            for p in places(half)
        ]
    )
    rows = {0: own}
    state = [{} for _ in range(4)]
    arrived = []
    half_hidden = gate_weight.shape[1] // 2
    stays = z_hi == core

    def tie(*values):
        values = lax.optimization_barrier(values)
        return values if len(values) > 1 else values[0]

    def product(rows, weight):
        return jnp.dot(rows, weight, preferred_element_type=F32)

    def parted(mixed):
        away, kept = mixed[:64], mixed[64:]
        return jnp.where(stays, kept, away), jnp.where(stays, away, kept)

    def step(e, s):
        st = state[e]
        if s == -1:
            rows[e] = swap_x[e](tie(own))
        elif s == 0:
            both = tie(rows[e])
            terms = [product(both, w) for w in (gate_weight, up_weight)]
            send, *st["total"] = tie(jnp.stack([lifted(v[:64]) for v in terms]), *terms)
            st["flight"] = swap_core(send)
        elif s in (2, 3, 4):
            got = tie(st["flight"])
            part = slice(64, 128) if s == 2 else slice(0, got.shape[1])
            total = [v[part] + lowered(g) for v, g in zip(st["total"], got)]
            if e == Z_FIRST and s == 2:
                sides = [(v[:, :half_hidden], v[:, half_hidden:]) for v in total]
                send = jnp.stack([lifted(jnp.where(z_lo == 0, hi, lo)) for lo, hi in sides])
                total = [jnp.where(z_lo == 0, lo, hi) for lo, hi in sides]
                swap = swap_z
            else:
                over = s - 1 if e == Z_FIRST else s
                part = slice(0 if over == 4 else got.shape[1] // 2, None)
                send = jnp.stack([lifted(v[part]) for v in total])
                swap = (swap_first, swap_second, swap_z)[over - 2]
            send, *st["total"] = tie(send, *total)
            st["flight"] = swap(send)
        elif s == 5:
            got = tie(st["flight"])
            gate, up = [v[: got.shape[1]] + lowered(g) for v, g in zip(st["total"], got)]
            st["hidden"] = tie((jax.nn.silu(gate) * up).astype(BF16))
            if e == Z_FIRST:
                near, far = st["hidden"], tie(swap_z(st["hidden"]))
                sides = (jnp.where(z_lo == 0, near, far), jnp.where(z_lo == 0, far, near))
                st["hidden"] = tie(jnp.concatenate(sides, axis=1))
            st["flight"] = swap_second(st["hidden"])
        elif s in (6, 7):
            st["hidden"] = tie(jnp.concatenate((st["hidden"], tie(st["flight"]))))
            st["flight"] = (swap_first if s == 6 else swap_core)(st["hidden"])
        elif s == 8:
            both = jnp.concatenate((tie(st["flight"]), st["hidden"]))
            mixed = product(both, down_weight)
            if e == 0:
                whole.append(tie(mixed))
            elif e == 3:
                whole.append(swap_x[e](tie(mixed.astype(BF16))).astype(F32))
            else:
                same, cross = parted(mixed)
                same, cross = tie(same.astype(BF16), cross.astype(BF16))
                arrived.append(swap_x[e](same).astype(F32))
                arrived.append(swap_row[e](cross).astype(F32))

    whole = []
    for s in (-1, 0, 2, 3, 4, 5, 6, 7, 8):
        for e in (0, 2, 1, 3):
            if e or s >= 0:
                step(e, s)

    same, cross = parted(sum(whole))
    same, cross = tie(same, cross.astype(BF16))
    arrived += [same, swap_row[0](cross).astype(F32)]
    out = sum(arrived).astype(BF16).reshape(4, 16, -1)
    first = jnp.where(z_hi == 0, 1, 3)
    blocks = []
    for p in range(4):
        e = y ^ p
        place = jnp.where(e == 0, 0, jnp.where(e == 2, 3, jnp.where(e == first, 2, 1)))
        blocks.append(lax.dynamic_index_in_dim(out, place, 0, keepdims=False))
    return jnp.concatenate(blocks)


def solution(mesh):
    grid = Mesh(mesh.devices.reshape(4, 2, 4, 2, 2), AXES)
    row, col = AXES[:2], AXES[2:]
    placed = (P(AXES, None), P(col, row), P(col, row), P(row, col))
    return jax.shard_map(
        per_device, mesh=grid, in_specs=placed, out_specs=P(row, col), check_vma=False
    )
```

```python
import jax
import jax.numpy as jnp
from jax import lax
from jax.sharding import Mesh, PartitionSpec as P

F32, BF16, F16 = jnp.float32, jnp.bfloat16, jnp.float16
LIFT = 8.0
AXES = ("x", "z_hi", "y", "z_lo", "core")
Z_FIRST = 3


def permute(axes, sizes, move):
    def flat(place):
        index = 0
        for size, part in zip(sizes, place):
            index = index * size + part
        return index

    places = [()]
    for size in sizes:
        places = [p + (i,) for p in places for i in range(size)]
    pairs = [(flat(p), flat(move(*p))) for p in places]
    return lambda v: lax.ppermute(v, axes, pairs)


def lifted(v):
    return (v * LIFT).astype(F16)


def lowered(v):
    return v.astype(F32) * (1 / LIFT)


def per_device(tokens, gate_weight, up_weight, down_weight):
    z_hi, y, z_lo, core = (lax.axis_index(a) for a in AXES[1:])
    swap_core = permute(("core",), (2,), lambda c: (c ^ 1,))
    swap_z = permute(("z_lo",), (2,), lambda z: (z ^ 1,))
    swap_first = permute(("y", "core"), (4, 2), lambda y, c: (y ^ (3 if c else 1), c))
    swap_second = permute(("y", "core"), (4, 2), lambda y, c: (y ^ (1 if c else 3), c))
    swap_x = {e: permute(("x",), (4,), lambda x, e=e: (x ^ e,)) for e in (1, 2, 3)}
    swap_row = {
        e: permute(("x", "z_hi"), (4, 2), lambda x, z, e=e: (x ^ e, z ^ 1)) for e in range(3)
    }

    features = tokens.shape[1] // 16
    blocks = tokens.reshape(4, 16, features).transpose(1, 0, 2)
    blocks = jnp.concatenate((blocks, blocks))
    mine = lax.all_to_all(blocks, AXES[1:], split_axis=0, concat_axis=0, tiled=True)
    mine = mine.reshape(2, 4, 16, features)

    def places(half):
        first = jnp.where(half == 0, 1, 3)
        return (y, y ^ (4 - first), y ^ first, y ^ 2)

    halves = (1 - core, core)
    own = jnp.concatenate(
        [
            lax.dynamic_slice(mine, (half, p, 0, 0), (1, 1, 16, features)).reshape(16, features)
            for half in halves
            for p in places(half)
        ]
    )
    rows = {0: own}
    state = [{} for _ in range(4)]
    arrived = []
    half_hidden = gate_weight.shape[1] // 2
    stays = z_hi == core

    def tie(*values):
        values = lax.optimization_barrier(values)
        return values if len(values) > 1 else values[0]

    def product(rows, weight):
        return jnp.dot(rows, weight, preferred_element_type=F32)

    def parted(mixed):
        away, kept = mixed[:64], mixed[64:]
        return jnp.where(stays, kept, away), jnp.where(stays, away, kept)

    def step(e, s):
        st = state[e]
        if s == -1:
            rows[e] = swap_x[e](tie(own))
        elif s == 0:
            both = tie(rows[e])
            terms = [product(both, w) for w in (gate_weight, up_weight)]
            send, *st["total"] = tie(jnp.stack([lifted(v[:64]) for v in terms]), *terms)
            st["flight"] = swap_core(send)
        elif s in (2, 3, 4):
            got = tie(st["flight"])
            part = slice(64, 128) if s == 2 else slice(0, got.shape[1])
            total = [v[part] + lowered(g) for v, g in zip(st["total"], got)]
            if e == Z_FIRST and s == 2:
                sides = [(v[:, :half_hidden], v[:, half_hidden:]) for v in total]
                send = jnp.stack([lifted(jnp.where(z_lo == 0, hi, lo)) for lo, hi in sides])
                total = [jnp.where(z_lo == 0, lo, hi) for lo, hi in sides]
                swap = swap_z
            else:
                over = s - 1 if e == Z_FIRST else s
                part = slice(0 if over == 4 else got.shape[1] // 2, None)
                send = jnp.stack([lifted(v[part]) for v in total])
                swap = (swap_first, swap_second, swap_z)[over - 2]
            send, *st["total"] = tie(send, *total)
            st["flight"] = swap(send)
        elif s == 5:
            got = tie(st["flight"])
            gate, up = [v[: got.shape[1]] + lowered(g) for v, g in zip(st["total"], got)]
            st["hidden"] = tie((jax.nn.silu(gate) * up).astype(BF16))
            if e == Z_FIRST:
                near, far = st["hidden"], tie(swap_z(st["hidden"]))
                sides = (jnp.where(z_lo == 0, near, far), jnp.where(z_lo == 0, far, near))
                st["hidden"] = tie(jnp.concatenate(sides, axis=1))
            st["flight"] = swap_second(st["hidden"])
        elif s in (6, 7):
            st["hidden"] = tie(jnp.concatenate((st["hidden"], tie(st["flight"]))))
            st["flight"] = (swap_first if s == 6 else swap_core)(st["hidden"])
        elif s == 8:
            both = jnp.concatenate((tie(st["flight"]), st["hidden"]))
            mixed = product(both, down_weight)
            if e == 0:
                whole.append(tie(mixed))
            elif e == 3:
                whole.append(swap_x[e](tie(mixed.astype(BF16))).astype(F32))
            else:
                same, cross = parted(mixed)
                same, cross = tie(same.astype(BF16), cross.astype(BF16))
                arrived.append(swap_x[e](same).astype(F32))
                arrived.append(swap_row[e](cross).astype(F32))

    whole = []
    for s in (-1, 0, 2, 3, 4, 5, 6, 7, 8):
        for e in (0, 2, 1, 3):
            if e or s >= 0:
                step(e, s)

    same, cross = parted(sum(whole))
    same, cross = tie(same, cross.astype(BF16))
    arrived += [same, swap_row[0](cross).astype(F32)]
    out = sum(arrived).astype(BF16).reshape(4, 16, -1)
    first = jnp.where(z_hi == 0, 1, 3)
    blocks = []
    for p in range(4):
        e = y ^ p
        place = jnp.where(e == 0, 0, jnp.where(e == 2, 3, jnp.where(e == first, 2, 1)))
        blocks.append(lax.dynamic_index_in_dim(out, place, 0, keepdims=False))
    return jnp.concatenate(blocks)


def solution(mesh):
    grid = Mesh(mesh.devices.reshape(4, 2, 4, 2, 2), AXES)
    row, col = AXES[:2], AXES[2:]
    placed = (P(AXES, None), P(col, row), P(col, row), P(row, col))
    return jax.shard_map(
        per_device, mesh=grid, in_specs=placed, out_specs=P(row, col), check_vma=False
    )
```

```python
import jax
import jax.numpy as jnp
from jax import lax
from jax.sharding import Mesh, PartitionSpec as P

F32, BF16, F16 = jnp.float32, jnp.bfloat16, jnp.float16
LIFT = 8.0
AXES = ("x", "z_hi", "y", "z_lo", "core")
Z_FIRST = 1


def permute(axes, sizes, move):
    def flat(place):
        index = 0
        for size, part in zip(sizes, place):
            index = index * size + part
        return index

    places = [()]
    for size in sizes:
        places = [p + (i,) for p in places for i in range(size)]
    pairs = [(flat(p), flat(move(*p))) for p in places]
    return lambda v: lax.ppermute(v, axes, pairs)


def lifted(v):
    return (v * LIFT).astype(F16)


def lowered(v):
    return v.astype(F32) * (1 / LIFT)


def per_device(tokens, gate_weight, up_weight, down_weight):
    z_hi, y, z_lo, core = (lax.axis_index(a) for a in AXES[1:])
    swap_core = permute(("core",), (2,), lambda c: (c ^ 1,))
    swap_z = permute(("z_lo",), (2,), lambda z: (z ^ 1,))
    swap_first = permute(("y", "core"), (4, 2), lambda y, c: (y ^ (3 if c else 1), c))
    swap_second = permute(("y", "core"), (4, 2), lambda y, c: (y ^ (1 if c else 3), c))
    swap_x = {e: permute(("x",), (4,), lambda x, e=e: (x ^ e,)) for e in (1, 2, 3)}
    swap_row = {
        e: permute(("x", "z_hi"), (4, 2), lambda x, z, e=e: (x ^ e, z ^ 1)) for e in (0, 2, 3)
    }

    features = tokens.shape[1] // 16
    blocks = tokens.reshape(4, 16, features).transpose(1, 0, 2).reshape(1, 64, features)
    blocks = jnp.broadcast_to(blocks, (2, 64, features)).reshape(128, features)
    mine = lax.all_to_all(blocks, AXES[1:], split_axis=0, concat_axis=0, tiled=True)
    mine = mine.reshape(2, 4, 16, features)

    def places(half):
        first = jnp.where(half == 0, 1, 3)
        return (y, y ^ (4 - first), y ^ first, y ^ 2)

    halves = (1 - core, core)
    own = jnp.concatenate(
        [
            lax.dynamic_slice(mine, (half, p, 0, 0), (1, 1, 16, features)).reshape(16, features)
            for half in halves
            for p in places(half)
        ]
    )
    rows = {0: own}
    state = [{} for _ in range(4)]
    arrived = []
    half_hidden = gate_weight.shape[1] // 2
    stays = z_hi == core

    def tie(*values):
        values = lax.optimization_barrier(values)
        return values if len(values) > 1 else values[0]

    def product(rows, weight):
        return jnp.dot(rows, weight, preferred_element_type=F32)

    def parted(mixed):
        away, kept = mixed[:64], mixed[64:]
        return jnp.where(stays, kept, away), jnp.where(stays, away, kept)

    def step(e, s):
        st = state[e]
        if s == -1:
            rows[e] = swap_x[e](tie(own))
        elif s == 0:
            both = tie(rows[e])
            terms = [product(both, w) for w in (gate_weight, up_weight)]
            send, *st["total"] = tie(jnp.stack([lifted(v[:64]) for v in terms]), *terms)
            st["flight"] = swap_core(send)
        elif s in (2, 3, 4):
            got = tie(st["flight"])
            part = slice(64, 128) if s == 2 else slice(0, got.shape[1])
            total = [v[part] + lowered(g) for v, g in zip(st["total"], got)]
            if e == Z_FIRST and s == 2:
                sides = [(v[:, :half_hidden], v[:, half_hidden:]) for v in total]
                send = jnp.stack([lifted(jnp.where(z_lo == 0, hi, lo)) for lo, hi in sides])
                total = [jnp.where(z_lo == 0, lo, hi) for lo, hi in sides]
                swap = swap_z
            else:
                over = s - 1 if e == Z_FIRST else s
                part = slice(0 if over == 4 else got.shape[1] // 2, None)
                send = jnp.stack([lifted(v[part]) for v in total])
                swap = (swap_first, swap_second, swap_z)[over - 2]
            send, *st["total"] = tie(send, *total)
            st["flight"] = swap(send)
        elif s == 5:
            got = tie(st["flight"])
            gate, up = [v[: got.shape[1]] + lowered(g) for v, g in zip(st["total"], got)]
            st["hidden"] = tie((jax.nn.silu(gate) * up).astype(BF16))
            if e == Z_FIRST:
                near, far = st["hidden"], tie(swap_z(st["hidden"]))
                sides = (jnp.where(z_lo == 0, near, far), jnp.where(z_lo == 0, far, near))
                st["hidden"] = tie(jnp.concatenate(sides, axis=1))
            st["flight"] = swap_second(st["hidden"])
        elif s in (6, 7):
            st["hidden"] = tie(jnp.concatenate((st["hidden"], tie(st["flight"]))))
            st["flight"] = (swap_first if s == 6 else swap_core)(st["hidden"])
        elif s == 8:
            both = jnp.concatenate((tie(st["flight"]), st["hidden"]))
            mixed = product(both, down_weight)
            if e == 0:
                whole.append(tie(mixed))
            elif e == 1:
                whole.append(swap_x[e](tie(mixed.astype(BF16))).astype(F32))
            else:
                same, cross = parted(mixed)
                same, cross = tie(same.astype(BF16), cross.astype(BF16))
                arrived.append(swap_x[e](same).astype(F32))
                arrived.append(swap_row[e](cross).astype(F32))

    whole = []
    for s in (-1, 0, 2, 3, 4, 5, 6, 7, 8):
        for e in (0, 2, 3, 1):
            if e or s >= 0:
                step(e, s)

    same, cross = parted(sum(whole))
    same, cross = tie(same, cross.astype(BF16))
    arrived += [same, swap_row[0](cross).astype(F32)]
    out = sum(arrived).astype(BF16).reshape(4, 16, -1)
    first = jnp.where(z_hi == 0, 1, 3)
    blocks = []
    for p in range(4):
        e = y ^ p
        place = jnp.where(e == 0, 0, jnp.where(e == 2, 3, jnp.where(e == first, 2, 1)))
        blocks.append(lax.dynamic_index_in_dim(out, place, 0, keepdims=False))
    return jnp.concatenate(blocks)


def solution(mesh):
    grid = Mesh(mesh.devices.reshape(4, 2, 4, 2, 2), AXES)
    row, col = AXES[:2], AXES[2:]
    placed = (P(AXES, None), P(col, row), P(col, row), P(row, col))
    return jax.shard_map(
        per_device, mesh=grid, in_specs=placed, out_specs=P(row, col), check_vma=False
    )
```

```python
import jax
import jax.numpy as jnp
from jax import lax
from jax.sharding import Mesh, PartitionSpec as P

F32, BF16, F16 = jnp.float32, jnp.bfloat16, jnp.float16
LIFT = 8.0
AXES = ("x", "z_hi", "y", "z_lo", "core")
Z_FIRST = 3


def permute(axes, sizes, move):
    def flat(place):
        index = 0
        for size, part in zip(sizes, place):
            index = index * size + part
        return index

    places = [()]
    for size in sizes:
        places = [p + (i,) for p in places for i in range(size)]
    pairs = [(flat(p), flat(move(*p))) for p in places]
    return lambda v: lax.ppermute(v, axes, pairs)


def lifted(v):
    return (v * LIFT).astype(F16)


def lowered(v):
    return v.astype(F32) * (1 / LIFT)


def per_device(tokens, gate_weight, up_weight, down_weight):
    z_hi, y, z_lo, core = (lax.axis_index(a) for a in AXES[1:])
    swap_core = permute(("core",), (2,), lambda c: (c ^ 1,))
    swap_z = permute(("z_lo",), (2,), lambda z: (z ^ 1,))
    swap_first = permute(("y", "core"), (4, 2), lambda y, c: (y ^ (3 if c else 1), c))
    swap_second = permute(("y", "core"), (4, 2), lambda y, c: (y ^ (1 if c else 3), c))
    swap_x = {e: permute(("x",), (4,), lambda x, e=e: (x ^ e,)) for e in (1, 2, 3)}
    swap_row = {
        e: permute(("x", "z_hi"), (4, 2), lambda x, z, e=e: (x ^ e, z ^ 1)) for e in range(3)
    }

    features = tokens.shape[1] // 16
    blocks = tokens.reshape(4, 16, features).transpose(1, 0, 2).reshape(1, 64, features)
    blocks = jnp.broadcast_to(blocks, (2, 64, features)).reshape(128, features)
    mine = lax.all_to_all(blocks, AXES[1:], split_axis=0, concat_axis=0, tiled=True)
    mine = mine.reshape(2, 4, 16, features)

    def places(half):
        first = jnp.where(half == 0, 1, 3)
        return (y, y ^ (4 - first), y ^ first, y ^ 2)

    halves = (1 - core, core)
    own = jnp.concatenate(
        [
            lax.dynamic_slice(mine, (half, p, 0, 0), (1, 1, 16, features)).reshape(16, features)
            for half in halves
            for p in places(half)
        ]
    )
    rows = {0: own}
    state = [{} for _ in range(4)]
    arrived = []
    half_hidden = gate_weight.shape[1] // 2
    stays = z_hi == core

    def tie(*values):
        values = lax.optimization_barrier(values)
        return values if len(values) > 1 else values[0]

    def product(rows, weight):
        return jnp.dot(rows, weight, preferred_element_type=F32)

    def parted(mixed):
        away, kept = mixed[:64], mixed[64:]
        return jnp.where(stays, kept, away), jnp.where(stays, away, kept)

    def step(e, s):
        st = state[e]
        if s == -1:
            rows[e] = swap_x[e](tie(own))
        elif s == 0:
            both = tie(rows[e])
            terms = [product(both, w) for w in (gate_weight, up_weight)]
            send, *st["total"] = tie(jnp.stack([lifted(v[:64]) for v in terms]), *terms)
            st["flight"] = swap_core(send)
        elif s in (2, 3, 4):
            got = tie(st["flight"])
            part = slice(64, 128) if s == 2 else slice(0, got.shape[1])
            total = [v[part] + lowered(g) for v, g in zip(st["total"], got)]
            if e == Z_FIRST and s == 2:
                sides = [(v[:, :half_hidden], v[:, half_hidden:]) for v in total]
                send = jnp.stack([lifted(jnp.where(z_lo == 0, hi, lo)) for lo, hi in sides])
                total = [jnp.where(z_lo == 0, lo, hi) for lo, hi in sides]
                swap = swap_z
            else:
                over = s - 1 if e == Z_FIRST else s
                part = slice(0 if over == 4 else got.shape[1] // 2, None)
                send = jnp.stack([lifted(v[part]) for v in total])
                swap = (swap_first, swap_second, swap_z)[over - 2]
            send, st["total"] = tie(send), total
            st["flight"] = swap(send)
        elif s == 5:
            got = tie(st["flight"])
            gate, up = [v[: got.shape[1]] + lowered(g) for v, g in zip(st["total"], got)]
            st["hidden"] = tie((jax.nn.silu(gate) * up).astype(BF16))
            if e == Z_FIRST:
                near, far = st["hidden"], tie(swap_z(st["hidden"]))
                sides = (jnp.where(z_lo == 0, near, far), jnp.where(z_lo == 0, far, near))
                st["hidden"] = tie(jnp.concatenate(sides, axis=1))
            st["flight"] = swap_second(st["hidden"])
        elif s in (6, 7):
            st["hidden"] = tie(jnp.concatenate((st["hidden"], tie(st["flight"]))))
            st["flight"] = (swap_first if s == 6 else swap_core)(st["hidden"])
        elif s == 8:
            both = jnp.concatenate((tie(st["flight"]), st["hidden"]))
            mixed = product(both, down_weight)
            if e == 0:
                whole.append(tie(mixed))
            elif e == 3:
                whole.append(swap_x[e](tie(mixed.astype(BF16))).astype(F32))
            else:
                same, cross = parted(mixed)
                same, cross = tie(same.astype(BF16), cross.astype(BF16))
                arrived.append(swap_x[e](same).astype(F32))
                arrived.append(swap_row[e](cross).astype(F32))

    whole = []
    for s in (-1, 0, 2, 3, 4, 5, 6, 7, 8):
        for e in (0, 2, 1, 3):
            if e or s >= 0:
                step(e, s)

    same, cross = parted(sum(whole))
    same, cross = tie(same, cross.astype(BF16))
    arrived += [same, swap_row[0](cross).astype(F32)]
    out = sum(arrived).astype(BF16).reshape(4, 16, -1)
    first = jnp.where(z_hi == 0, 1, 3)
    blocks = []
    for p in range(4):
        e = y ^ p
        place = jnp.where(e == 0, 0, jnp.where(e == 2, 3, jnp.where(e == first, 2, 1)))
        blocks.append(lax.dynamic_index_in_dim(out, place, 0, keepdims=False))
    return jnp.concatenate(blocks)


def solution(mesh):
    grid = Mesh(mesh.devices.reshape(4, 2, 4, 2, 2), AXES)
    row, col = AXES[:2], AXES[2:]
    placed = (P(AXES, None), P(col, row), P(col, row), P(row, col))
    return jax.shard_map(
        per_device, mesh=grid, in_specs=placed, out_specs=P(row, col), check_vma=False
    )
```
